32 devices in a mesh: groups: 2 (over y), expert: 4 (over z), head: 4 (over x, core).
Axes of the slice: x: 2, y: 2, z: 4, core: 2. Of those that a mesh axis runs over, the one named last changes fastest.
Arguments:
- tokens: bfloat16 [2, 32, 7168], P(None, ('groups', 'expert'), 'head'), parts along dimension 1, may hold values from -6 to 6
- gate_scores: float32 [2, 32, 2], P(None, ('groups', 'expert')), parts along dimension 1, may hold values from 0.05 to 1
- route_copy: int32 [2, 32, 2], P(None, ('groups', 'expert')), parts along dimension 1, may hold values from 0 to 3, as said below
- gate_up: bfloat16 [4, 7168, 2, 1024], P('expert', 'head'), as said below
- down_proj: bfloat16 [4, 1024, 7168], P('expert', None, 'head')
Outputs:
- combined: bfloat16 [2, 32, 7168], P(None, ('groups', 'expert'), 'head'), parts along dimension 1
The draws below stay inside these ranges and needn't reach their ends.
There are 2 independent parts, one for each index of `groups`. The reference program is written for one: setup_inputs(seed, part) draws one part's arguments, and reference() takes and returns one part's arrays. A program takes and returns all parts, laid end to end along the dimension named above; an argument that names none is the same for every part. Nothing has to cross between parts.
Inputs may be any that keep to these rules, and one draw needn't show every extreme that they name: Each of the 3 experts is held by one or two slots; slots that hold the same expert hold equal projections in gate_up and down_proj. `route_copy`: the 2 copies named by one row are different. In one step, at most 4 entries of the rows of one index of expert name the same copy; in every draw some copies receive exactly 4 entries from the rows of every index of expert.
All inputs are finite; a program needn't handle non-finite values.
Results may differ from the reference program's by a relative error of at most 0.0049.
Values may be sent and summed in bfloat16 or wider, within the bound.
A program may use at most 64 MiB of HBM per device.

```python
import math
import jax
import jax.numpy as jnp
from jax import lax

D = 7168
FF = 1024
ROW_DEV = 4
STEPS = 2
SPAN = 1
SLOTS = 4
TOP = 2
EXPERTS = 3
PER = 4
ROWS = 16


def plan_slots(key):
    k_pick, k_place = jax.random.split(key)
    spare = jax.random.permutation(k_pick, EXPERTS)[:SLOTS - EXPERTS].astype(jnp.int32)
    listed = jnp.concatenate([jnp.arange(EXPERTS, dtype=jnp.int32), spare])
    order = jax.random.permutation(k_place, SLOTS).astype(jnp.int32)
    return jnp.zeros((SLOTS,), jnp.int32).at[order].set(listed)


def draw_gate_up(key, part):
    held = plan_slots(key)
    key = jax.random.fold_in(key, 7)

    def one_slot(expert):
        return jax.random.normal(jax.random.fold_in(key, expert), (D, 2, FF), jnp.float32)
    full = jax.vmap(one_slot)(held) * D ** (-0.5)
    full = full.reshape(SLOTS, D, 2, SPAN, FF // SPAN)
    full = jnp.transpose(full, (0, 3, 1, 2, 4)).reshape(SLOTS * SPAN, D, 2, FF // SPAN)
    return full.astype(jnp.bfloat16)


def draw_down_proj(key, part):
    held = plan_slots(key)
    key = jax.random.fold_in(key, 11)

    def one_slot(expert):
        return jax.random.normal(jax.random.fold_in(key, expert), (FF, D), jnp.float32)
    full = jax.vmap(one_slot)(held) * FF ** (-0.5)
    return full.reshape(SLOTS * SPAN, FF // SPAN, D).astype(jnp.bfloat16)


def draw_route_copy(key, part):
    key = jax.random.fold_in(key, 13)
    sources = ROWS // ROW_DEV
    members = SLOTS // TOP
    seat_count = 2 * ROW_DEV

    def group_seats(seat_key):
        return jax.random.permutation(seat_key, seat_count).astype(jnp.int32)[:ROW_DEV]

    def one_source(index):
        base_key = jax.random.fold_in(key, index)
        order_key, seat_key, rest_key, rows_key = jax.random.split(base_key, 4)
        order = jax.random.permutation(order_key, SLOTS).astype(jnp.int32)
        seats = jax.vmap(group_seats)(jax.random.split(seat_key, TOP))
        rest = PER + jax.random.permutation(rest_key, seat_count - PER).astype(jnp.int32)
        forced = jnp.concatenate([jnp.arange(PER, dtype=jnp.int32), rest[:ROW_DEV - PER]])
        forced = forced[jax.random.permutation(rows_key, ROW_DEV).astype(jnp.int32)]
        seats = seats.at[0].set(forced)
        places = jnp.arange(TOP, dtype=jnp.int32)[:, None] * members + seats // PER
        return jnp.transpose(order[places], (1, 0))
    picked = jax.vmap(one_source)(jnp.arange(STEPS * sources, dtype=jnp.int32))
    return picked.reshape(STEPS, ROWS, TOP)


def steps_of(own_key, dims, cuts, low, top_value):
    def one(dim, shards_of):
        steps = jax.random.uniform(jax.random.fold_in(jax.random.fold_in(own_key, 6), dim), (shards_of,), jnp.float32, low / len(cuts), top_value / len(cuts))
        return jnp.repeat(jnp.exp(steps), dims[dim] // shards_of).reshape((-1,) + (1,) * (len(dims) - dim - 1))

    loudness = one(*cuts[0])
    for cut in cuts[1:]:
        loudness = loudness * one(*cut)
    return loudness


def bell_draw(stream_key, shape, deviation, most, cuts=(), kind=jnp.bfloat16):
    level = steps_of(stream_key, shape, cuts, -0.22, 0.18) if cuts else 1.0
    values = jax.random.normal(stream_key, shape, jnp.float32) * deviation * level
    return jnp.minimum(jnp.maximum(values, -most), most).astype(kind)


def setup_inputs(seed: int = 0, part: int = 0) -> dict:
    streams_of = jax.random.split(jax.random.key(seed), 6)
    own_keys = jax.random.split(jax.random.fold_in(streams_of[5], part), 6)
    return {
        "tokens": bell_draw(own_keys[0], (STEPS, ROWS, D), 1.0, 6.0, ((1, 4), (2, 4))),
        "gate_scores": jnp.clip(jnp.exp(math.log(1.0) - 2.9957323 * jax.random.uniform(own_keys[1], (STEPS, ROWS, TOP), jnp.float32) ** steps_of(own_keys[1], (STEPS, ROWS, TOP), ((1, 4),), -0.2, 0.2)), 0.05, 1.0),
        "route_copy": draw_route_copy(jax.random.fold_in(jax.random.fold_in(streams_of[5], part), 71), part),
        "gate_up": draw_gate_up(jax.random.fold_in(streams_of[5], 71), part),
        "down_proj": draw_down_proj(jax.random.fold_in(streams_of[5], 71), part),
    }


def reference(tokens, gate_scores, route_copy, gate_up, down_proj):
    flat_tokens = tokens.reshape(STEPS * ROWS, D)
    weights = 2.5 * gate_scores / jnp.sum(gate_scores, axis=2, keepdims=True)
    weights = weights.reshape(STEPS * ROWS, TOP)
    copy_ids = route_copy.reshape(STEPS * ROWS, TOP)
    stacked_in = gate_up.reshape(SLOTS, SPAN, D, 2, FF // SPAN)
    stacked_out = down_proj.reshape(SLOTS, FF, D)

    def one_copy(total, copy_index):
        block = stacked_in[copy_index]
        w_in = jnp.transpose(block, (1, 2, 0, 3)).reshape(D, 2 * FF)
        gated = jnp.dot(flat_tokens, w_in, preferred_element_type=jnp.float32)
        hidden = (jax.nn.silu(gated[:, :FF]) * gated[:, FF:]).astype(jnp.bfloat16)
        result = jnp.dot(hidden, stacked_out[copy_index], preferred_element_type=jnp.float32)
        share = jnp.sum(jnp.where(copy_ids == copy_index, weights, 0.0), axis=1)
        return total + share[:, None] * result, None

    start = jnp.zeros((STEPS * ROWS, D), jnp.float32)
    total, unused = lax.scan(one_copy, start, jnp.arange(SLOTS, dtype=jnp.int32))
    return total.reshape(STEPS, ROWS, D).astype(jnp.bfloat16)
```

```python
import functools

import jax
import jax.numpy as jnp
from jax import lax
from jax.experimental import pallas as pl
from jax.experimental.pallas import tpu as pltpu
from jax.sharding import PartitionSpec as P

MESH = pl.DeviceIdType.MESH
F32, BF16 = jnp.float32, jnp.bfloat16


def widths_of(half):
    first = ((half // 128 + 1) // 2) * 128
    return [w for w in (first, half - first) if w]


def fused(
    experts,
    heads,
    span,
    tokens_ref,
    scores_ref,
    routes_ref,
    gate_up_ref,
    down_ref,
    out_ref,
    w_in,
    w_pairs,
    w_out,
    flat,
    packed,
    spread,
    share,
    sums,
    sums_out,
    sums_in,
    hidden_all,
    own,
    *rest,
):
    parts = (len(rest) - 10) // 2
    results_out, results_in = rest[:parts], rest[parts : 2 * parts]
    (w_sem, down_sem, tok_send, tok_recv, sum_send, sum_recv, hid_send, hid_recv, res_send, res_recv) = rest[2 * parts :]
    steps, rows, width = tokens_ref.shape
    half = width // 2
    count = steps * rows
    tiles = w_in.shape[0]
    units = tiles * 128
    chunks = w_pairs.shape[0]
    per_send = sums_out.shape[3] // 256
    groups = experts // heads
    me = lax.axis_index("expert")
    my_head = lax.axis_index("head")

    weight_copies = [
        pltpu.make_async_copy(gate_up_ref.at[:, 2 * c : 2 * c + 2, :], w_in.at[c], w_sem.at[c]) for c in range(tiles)
    ]
    for copy in weight_copies:
        copy.start()

    barrier = pltpu.get_barrier_semaphore()
    for o in range(1, experts):
        pl.semaphore_signal(barrier, inc=1, device_id={"expert": lax.rem(me + o, experts)}, device_id_type=MESH)
    for o in range(1, heads):
        pl.semaphore_signal(barrier, inc=1, device_id={"head": lax.rem(my_head + o, heads)}, device_id_type=MESH)

    for s in range(steps):
        flat[s * rows : (s + 1) * rows, :] = tokens_ref[s].astype(F32)
    packed[0] = jnp.concatenate([flat[:, :half], flat[:, half:]], axis=0).astype(BF16)

    pl.semaphore_wait(barrier, experts + heads - 2)

    token_copies = []
    for o in range(1, experts):
        copy = pltpu.make_async_remote_copy(
            src_ref=packed.at[0],
            dst_ref=packed.at[o],
            send_sem=tok_send.at[o],
            recv_sem=tok_recv.at[o],
            device_id={"expert": lax.rem(me + o, experts)},
            device_id_type=MESH,
        )
        copy.start()
        token_copies.append(copy)

    eye = lax.broadcasted_iota(jnp.int32, (rows, rows), 0) == lax.broadcasted_iota(jnp.int32, (rows, rows), 1)
    for s in range(steps):
        scores = scores_ref[s]
        weights = 2.5 * scores / jnp.sum(scores, axis=0, keepdims=True)
        for b in range(experts):
            slot = lax.rem(me + b, experts) // span
            row = jnp.sum(jnp.where(routes_ref[s] == slot, weights, 0.0), axis=0, keepdims=True)
            column = jnp.sum(jnp.where(eye, jnp.broadcast_to(row, (rows, rows)), 0.0), axis=1, keepdims=True)
            column = jnp.broadcast_to(column, (rows, 128))
            share[b, s * rows : (s + 1) * rows, :] = column
            share[b, count + s * rows : count + (s + 1) * rows, :] = column

    for c in range(chunks):
        weight_copies[2 * c].wait()
        weight_copies[2 * c + 1].wait()
        w_pairs[c] = jnp.concatenate([w_in[2 * c + i].reshape(2 * width, 128) for i in range(2)], axis=1)
    down_copy = pltpu.make_async_copy(down_ref, w_out, down_sem)
    down_copy.start()

    lane = lax.broadcasted_iota(jnp.int32, (128, 512), 1)
    feature = lax.broadcasted_iota(jnp.int32, (128, 512), 0)
    place = jnp.where(lane < 256, 2 * feature, 2 * feature + 257)
    selector = jnp.where(lane == place, 1.0, 0.0).astype(BF16)
    per_half = half // 128
    for b in range(experts):
        if b:
            token_copies[b - 1].wait_recv()
        block = packed[b]
        stack = jnp.concatenate([block[:, 128 * j : 128 * j + 128] for j in range(per_half)], axis=0)
        wide = jnp.dot(stack, selector, preferred_element_type=F32)
        for j in range(per_half):
            for k in range(2):
                piece = wide[16 * j + 8 * k : 16 * j + 8 * k + 8]
                pair = jnp.concatenate([piece[:, :256], piece[:, 256:]], axis=0).astype(BF16)
                at = 256 * (k * per_half + j)
                spread[16 * b : 16 * b + 16, at : at + 256] = pair

    sum_copies = []
    for c in range(chunks):
        part = jnp.dot(spread[...], w_pairs[c], preferred_element_type=F32)
        part = part.reshape(heads, 16 * groups, 256)
        sums[:, :, 256 * c : 256 * c + 256] = part
        n, k = c // per_send, c % per_send
        sums_out[:, n, :, 256 * k : 256 * k + 256] = part.astype(BF16)
        if k == per_send - 1:
            for o in range(1, heads):
                peer = lax.rem(my_head + o, heads)
                copy = pltpu.make_async_remote_copy(
                    src_ref=sums_out.at[peer, n],
                    dst_ref=sums_in.at[o - 1, n],
                    send_sem=sum_send.at[o - 1, n],
                    recv_sem=sum_recv.at[o - 1, n],
                    device_id={"head": peer},
                    device_id_type=MESH,
                )
                copy.start()
                sum_copies.append(copy)

    for copy in sum_copies:
        copy.wait_recv()
    sends = sums_out.shape[1]
    total = sums[my_head]
    for o in range(1, heads):
        total += jnp.concatenate([sums_in[o - 1, n].astype(F32) for n in range(sends)], axis=1)
    total = total.reshape(groups, 2, 8, units)
    gate, up = total[:, 0], total[:, 1]
    hidden = gate / (1.0 + jnp.exp(-gate)) * up
    hidden = jnp.stack([hidden[:, :, : units // 2], hidden[:, :, units // 2 :]], axis=1)
    hidden_all[my_head] = hidden.reshape(16 * groups, units // 2).astype(BF16)
    hidden_copies = []
    for o in range(1, heads):
        copy = pltpu.make_async_remote_copy(
            src_ref=hidden_all.at[my_head],
            dst_ref=hidden_all.at[my_head],
            send_sem=hid_send.at[o - 1],
            recv_sem=hid_recv.at[o - 1],
            device_id={"head": lax.rem(my_head + o, heads)},
            device_id_type=MESH,
        )
        copy.start()
        hidden_copies.append(copy)
    down_copy.wait()
    for copy in hidden_copies:
        copy.wait_recv()

    blocks = hidden_all[...].astype(F32).reshape(experts, 2, 8, units // 2)
    left = jnp.concatenate([blocks[:, 0], blocks[:, 1]], axis=2).reshape(8 * experts, units).astype(BF16)
    result_copies = []
    at = 0
    for n in range(parts):
        size = results_out[n].shape[2]
        low = jnp.dot(left, w_out[:, at : at + size], preferred_element_type=F32)
        high = jnp.dot(left, w_out[:, half + at : half + at + size], preferred_element_type=F32)
        both = jnp.concatenate([low.reshape(experts, 8, size), high.reshape(experts, 8, size)], axis=1)
        own[:, at : at + size] = both[0]
        results_out[n][...] = both.astype(BF16)
        for b in range(1, experts):
            copy = pltpu.make_async_remote_copy(
                src_ref=results_out[n].at[b],
                dst_ref=results_in[n].at[b],
                send_sem=res_send.at[b, n],
                recv_sem=res_recv.at[b, n],
                device_id={"expert": lax.rem(me - b + experts, experts)},
                device_id_type=MESH,
            )
            copy.start()
            result_copies.append(copy)
        at += size

    at = 0
    for n in range(parts):
        size = results_out[n].shape[2]
        mixed = share[0][:, :1] * own[:, at : at + size]
        for b in range(1, experts):
            result_copies[n * (experts - 1) + b - 1].wait_recv()
            mixed += share[b][:, :1] * results_in[n][b].astype(F32)
        for s in range(steps):
            for k in range(2):
                rows_at = k * count + s * rows
                to = k * half + at
                out_ref[s, :, to : to + size] = mixed[rows_at : rows_at + rows].astype(BF16)
        at += size

    for copy in token_copies + sum_copies + hidden_copies + result_copies:
        copy.wait_send()


def body(experts, heads, tokens, gate_scores, route_copy, gate_up, down_proj):
    steps, rows, width = tokens.shape
    units = gate_up.shape[3]
    span = max(1, experts // 16)
    count = steps * rows
    half = width // 2
    tiles = units // 128
    chunks = units // 256
    groups = experts // heads
    per_send = min(2, chunks)
    sends = chunks // per_send
    assert count == 8 and experts % heads == 0 and units % 256 == 0 and half % 128 == 0
    gate_up = gate_up.reshape(width, 2, tiles, 128).transpose(0, 2, 1, 3).reshape(width, 2 * tiles, 128)
    down = down_proj.reshape(units, width)
    parts = widths_of(half)
    vmem, hbm = pl.BlockSpec(memory_space=pltpu.VMEM), pl.BlockSpec(memory_space=pl.ANY)
    dma = pltpu.SemaphoreType.DMA
    flops = 2 * 8 * experts * width * units * 3
    return pl.pallas_call(
        functools.partial(fused, experts, heads, span),
        out_shape=jax.ShapeDtypeStruct(tokens.shape, tokens.dtype),
        in_specs=[vmem, vmem, vmem, hbm, hbm],
        out_specs=vmem,
        scratch_shapes=[
            pltpu.VMEM((tiles, width, 2, 128), BF16),
            pltpu.VMEM((chunks, 2 * width, 256), BF16),
            pltpu.VMEM((units, width), BF16),
            pltpu.VMEM((8, width), F32),
            pltpu.VMEM((experts, 16, half), BF16),
            pltpu.VMEM((16 * experts, 2 * width), BF16),
            pltpu.VMEM((experts, 16, 128), F32),
            pltpu.VMEM((heads, 16 * groups, units), F32),
            pltpu.VMEM((heads, sends, 16 * groups, 256 * per_send), BF16),
            pltpu.VMEM((heads - 1, sends, 16 * groups, 256 * per_send), BF16),
            pltpu.VMEM((heads, 16 * groups, units // 2), BF16),
            pltpu.VMEM((16, half), F32),
        ]
        + [pltpu.VMEM((experts, 16, size), BF16) for size in parts] * 2
        + [
            dma((tiles,)),
            dma,
            dma((experts,)),
            dma((experts,)),
            dma((heads - 1, sends)),
            dma((heads - 1, sends)),
            dma((heads - 1,)),
            dma((heads - 1,)),
            dma((experts, len(parts))),
            dma((experts, len(parts))),
        ],
        compiler_params=pltpu.CompilerParams(
            collective_id=0, has_side_effects=True, vmem_limit_bytes=56 * 2**20
        ),
        cost_estimate=pl.CostEstimate(
            flops=flops, bytes_accessed=6 * width * units, transcendentals=8 * groups * units
        ),
    )(tokens, gate_scores.transpose(0, 2, 1), route_copy.transpose(0, 2, 1), gate_up, down)


def solution(mesh):
    experts, heads = mesh.shape["expert"], mesh.shape["head"]
    return jax.shard_map(
        functools.partial(body, experts, heads),
        mesh=mesh,
        in_specs=(
            P(None, ("groups", "expert"), "head"),
            P(None, ("groups", "expert"), None),
            P(None, ("groups", "expert"), None),
            P("expert", "head", None, None),
            P("expert", None, "head"),
        ),
        out_specs=P(None, ("groups", "expert"), "head"),
        check_vma=False,
    )
```

```python
import functools

import jax
import jax.numpy as jnp
from jax import lax
from jax.experimental import pallas as pl
from jax.experimental.pallas import tpu as pltpu
from jax.sharding import PartitionSpec as P

MESH = pl.DeviceIdType.MESH
F32, BF16 = jnp.float32, jnp.bfloat16


def widths_of(half):
    first = ((half // 128 + 1) // 2) * 128
    return [w for w in (first, half - first) if w]


def fused(
    experts,
    heads,
    span,
    tokens_ref,
    scores_ref,
    routes_ref,
    gate_up_ref,
    down_ref,
    out_ref,
    w_in,
    w_pairs,
    w_out,
    flat,
    packed,
    spread,
    share,
    sums,
    sums_out,
    sums_in,
    hidden_all,
    own,
    tokens_in,
    scores_in,
    routes_in,
    *rest,
):
    parts = (len(rest) - 11) // 2
    results_out, results_in = rest[:parts], rest[parts : 2 * parts]
    (w_sem, down_sem, tok_send, tok_recv, sum_send, sum_recv, hid_send, hid_recv, res_send, res_recv, in_sem) = rest[2 * parts :]
    steps, rows, width = tokens_ref.shape
    half = width // 2
    count = steps * rows
    tiles = w_in.shape[0]
    units = tiles * 128
    chunks = w_pairs.shape[0]
    per_send = sums_out.shape[3] // 256
    groups = experts // heads
    me = lax.axis_index("expert")
    my_head = lax.axis_index("head")

    barrier = pltpu.get_barrier_semaphore()
    for o in range(1, experts):
        pl.semaphore_signal(barrier, inc=1, device_id={"expert": lax.rem(me + o, experts)}, device_id_type=MESH)
    for o in range(1, heads):
        pl.semaphore_signal(barrier, inc=1, device_id={"head": lax.rem(my_head + o, heads)}, device_id_type=MESH)

    small_copies = [
        pltpu.make_async_copy(src, dst, in_sem.at[n])
        for n, (src, dst) in enumerate(((tokens_ref, tokens_in), (scores_ref, scores_in), (routes_ref, routes_in)))
    ]
    for copy in small_copies:
        copy.start()
    weight_copies = [
        pltpu.make_async_copy(gate_up_ref.at[:, 2 * c : 2 * c + 2, :], w_in.at[c], w_sem.at[c]) for c in range(tiles)
    ]
    for copy in weight_copies:
        copy.start()

    small_copies[0].wait()
    for s in range(steps):
        flat[s * rows : (s + 1) * rows, :] = tokens_in[s].astype(F32)
    packed[0] = jnp.concatenate([flat[:, :half], flat[:, half:]], axis=0).astype(BF16)

    pl.semaphore_wait(barrier, experts + heads - 2)

    token_copies = []
    for o in range(1, experts):
        copy = pltpu.make_async_remote_copy(
            src_ref=packed.at[0],
            dst_ref=packed.at[o],
            send_sem=tok_send.at[o],
            recv_sem=tok_recv.at[o],
            device_id={"expert": lax.rem(me + o, experts)},
            device_id_type=MESH,
        )
        copy.start()
        token_copies.append(copy)

    small_copies[1].wait()
    small_copies[2].wait()
    eye = lax.broadcasted_iota(jnp.int32, (rows, rows), 0) == lax.broadcasted_iota(jnp.int32, (rows, rows), 1)
    for s in range(steps):
        scores = scores_in[s]
        weights = 2.5 * scores / jnp.sum(scores, axis=0, keepdims=True)
        for b in range(experts):
            slot = lax.rem(me + b, experts) // span
            row = jnp.sum(jnp.where(routes_in[s] == slot, weights, 0.0), axis=0, keepdims=True)
            column = jnp.sum(jnp.where(eye, jnp.broadcast_to(row, (rows, rows)), 0.0), axis=1, keepdims=True)
            column = jnp.broadcast_to(column, (rows, 128))
            share[b, s * rows : (s + 1) * rows, :] = column
            share[b, count + s * rows : count + (s + 1) * rows, :] = column

    for c in range(chunks):
        weight_copies[2 * c].wait()
        weight_copies[2 * c + 1].wait()
        w_pairs[c] = jnp.concatenate([w_in[2 * c + i].reshape(2 * width, 128) for i in range(2)], axis=1)
    down_copy = pltpu.make_async_copy(down_ref, w_out, down_sem)
    down_copy.start()

    lane = lax.broadcasted_iota(jnp.int32, (128, 512), 1)
    feature = lax.broadcasted_iota(jnp.int32, (128, 512), 0)
    place = jnp.where(lane < 256, 2 * feature, 2 * feature + 257)
    selector = jnp.where(lane == place, 1.0, 0.0).astype(BF16)
    per_half = half // 128
    for b in range(experts):
        if b:
            token_copies[b - 1].wait_recv()
        block = packed[b]
        stack = jnp.concatenate([block[:, 128 * j : 128 * j + 128] for j in range(per_half)], axis=0)
        wide = jnp.dot(stack, selector, preferred_element_type=F32)
        for j in range(per_half):
            for k in range(2):
                piece = wide[16 * j + 8 * k : 16 * j + 8 * k + 8]
                pair = jnp.concatenate([piece[:, :256], piece[:, 256:]], axis=0).astype(BF16)
                at = 256 * (k * per_half + j)
                spread[16 * b : 16 * b + 16, at : at + 256] = pair

    sum_copies = []
    for c in range(chunks):
        part = jnp.dot(spread[...], w_pairs[c], preferred_element_type=F32)
        part = part.reshape(heads, 16 * groups, 256)
        sums[:, :, 256 * c : 256 * c + 256] = part
        n, k = c // per_send, c % per_send
        sums_out[:, n, :, 256 * k : 256 * k + 256] = part.astype(BF16)
        if k == per_send - 1:
            for o in range(1, heads):
                peer = lax.rem(my_head + o, heads)
                copy = pltpu.make_async_remote_copy(
                    src_ref=sums_out.at[peer, n],
                    dst_ref=sums_in.at[o - 1, n],
                    send_sem=sum_send.at[o - 1, n],
                    recv_sem=sum_recv.at[o - 1, n],
                    device_id={"head": peer},
                    device_id_type=MESH,
                )
                copy.start()
                sum_copies.append(copy)

    for copy in sum_copies:
        copy.wait_recv()
    sends = sums_out.shape[1]
    total = sums[my_head]
    for o in range(1, heads):
        total += jnp.concatenate([sums_in[o - 1, n].astype(F32) for n in range(sends)], axis=1)
    total = total.reshape(groups, 2, 8, units)
    gate, up = total[:, 0], total[:, 1]
    hidden = gate / (1.0 + jnp.exp(-gate)) * up
    hidden = jnp.stack([hidden[:, :, : units // 2], hidden[:, :, units // 2 :]], axis=1)
    hidden_all[my_head] = hidden.reshape(16 * groups, units // 2).astype(BF16)
    hidden_copies = []
    for o in range(1, heads):
        copy = pltpu.make_async_remote_copy(
            src_ref=hidden_all.at[my_head],
            dst_ref=hidden_all.at[my_head],
            send_sem=hid_send.at[o - 1],
            recv_sem=hid_recv.at[o - 1],
            device_id={"head": lax.rem(my_head + o, heads)},
            device_id_type=MESH,
        )
        copy.start()
        hidden_copies.append(copy)
    down_copy.wait()
    for copy in hidden_copies:
        copy.wait_recv()

    blocks = hidden_all[...].astype(F32).reshape(experts, 2, 8, units // 2)
    left = jnp.concatenate([blocks[:, 0], blocks[:, 1]], axis=2).reshape(8 * experts, units).astype(BF16)
    result_copies = []
    at = 0
    for n in range(parts):
        size = results_out[n].shape[2]
        low = jnp.dot(left, w_out[:, at : at + size], preferred_element_type=F32)
        high = jnp.dot(left, w_out[:, half + at : half + at + size], preferred_element_type=F32)
        both = jnp.concatenate([low.reshape(experts, 8, size), high.reshape(experts, 8, size)], axis=1)
        own[:, at : at + size] = both[0]
        results_out[n][...] = both.astype(BF16)
        for b in range(1, experts):
            copy = pltpu.make_async_remote_copy(
                src_ref=results_out[n].at[b],
                dst_ref=results_in[n].at[b],
                send_sem=res_send.at[b, n],
                recv_sem=res_recv.at[b, n],
                device_id={"expert": lax.rem(me - b + experts, experts)},
                device_id_type=MESH,
            )
            copy.start()
            result_copies.append(copy)
        at += size

    at = 0
    for n in range(parts):
        size = results_out[n].shape[2]
        mixed = share[0][:, :1] * own[:, at : at + size]
        for b in range(1, experts):
            result_copies[n * (experts - 1) + b - 1].wait_recv()
            mixed += share[b][:, :1] * results_in[n][b].astype(F32)
        for s in range(steps):
            for k in range(2):
                rows_at = k * count + s * rows
                to = k * half + at
                out_ref[s, :, to : to + size] = mixed[rows_at : rows_at + rows].astype(BF16)
        at += size

    for copy in token_copies + sum_copies + hidden_copies + result_copies:
        copy.wait_send()


def body(experts, heads, tokens, gate_scores, route_copy, gate_up, down_proj):
    steps, rows, width = tokens.shape
    units = gate_up.shape[3]
    span = max(1, experts // 16)
    count = steps * rows
    half = width // 2
    tiles = units // 128
    chunks = units // 256
    groups = experts // heads
    per_send = min(2, chunks)
    sends = chunks // per_send
    assert count == 8 and experts % heads == 0 and units % 256 == 0 and half % 128 == 0
    gate_up = gate_up.reshape(width, 2, tiles, 128).transpose(0, 2, 1, 3).reshape(width, 2 * tiles, 128)
    down = down_proj.reshape(units, width)
    parts = widths_of(half)
    vmem, hbm = pl.BlockSpec(memory_space=pltpu.VMEM), pl.BlockSpec(memory_space=pl.ANY)
    dma = pltpu.SemaphoreType.DMA
    flops = 2 * 8 * experts * width * units * 3
    return pl.pallas_call(
        functools.partial(fused, experts, heads, span),
        out_shape=jax.ShapeDtypeStruct(tokens.shape, tokens.dtype),
        in_specs=[hbm] * 5,
        out_specs=vmem,
        scratch_shapes=[
            pltpu.VMEM((tiles, width, 2, 128), BF16),
            pltpu.VMEM((chunks, 2 * width, 256), BF16),
            pltpu.VMEM((units, width), BF16),
            pltpu.VMEM((8, width), F32),
            pltpu.VMEM((experts, 16, half), BF16),
            pltpu.VMEM((16 * experts, 2 * width), BF16),
            pltpu.VMEM((experts, 16, 128), F32),
            pltpu.VMEM((heads, 16 * groups, units), F32),
            pltpu.VMEM((heads, sends, 16 * groups, 256 * per_send), BF16),
            pltpu.VMEM((heads - 1, sends, 16 * groups, 256 * per_send), BF16),
            pltpu.VMEM((heads, 16 * groups, units // 2), BF16),
            pltpu.VMEM((16, half), F32),
            pltpu.VMEM(tokens.shape, BF16),
            pltpu.VMEM((steps, route_copy.shape[2], rows), F32),
            pltpu.VMEM((steps, route_copy.shape[2], rows), jnp.int32),
        ]
        + [pltpu.VMEM((experts, 16, size), BF16) for size in parts] * 2
        + [
            dma((tiles,)),
            dma,
            dma((experts,)),
            dma((experts,)),
            dma((heads - 1, sends)),
            dma((heads - 1, sends)),
            dma((heads - 1,)),
            dma((heads - 1,)),
            dma((experts, len(parts))),
            dma((experts, len(parts))),
            dma((3,)),
        ],
        compiler_params=pltpu.CompilerParams(
            collective_id=0, has_side_effects=True, vmem_limit_bytes=56 * 2**20
        ),
        cost_estimate=pl.CostEstimate(
            flops=flops, bytes_accessed=6 * width * units, transcendentals=8 * groups * units
        ),
    )(tokens, gate_scores.transpose(0, 2, 1), route_copy.transpose(0, 2, 1), gate_up, down)


def solution(mesh):
    experts, heads = mesh.shape["expert"], mesh.shape["head"]
    return jax.shard_map(
        functools.partial(body, experts, heads),
        mesh=mesh,
        in_specs=(
            P(None, ("groups", "expert"), "head"),
            P(None, ("groups", "expert"), None),
            P(None, ("groups", "expert"), None),
            P("expert", "head", None, None),
            P("expert", None, "head"),
        ),
        out_specs=P(None, ("groups", "expert"), "head"),
        check_vma=False,
    )
```

```python
import functools

import jax
import jax.numpy as jnp
from jax import lax
from jax.experimental import pallas as pl
from jax.experimental.pallas import tpu as pltpu
from jax.sharding import PartitionSpec as P

MESH = pl.DeviceIdType.MESH
F32, BF16 = jnp.float32, jnp.bfloat16


def widths_of(half):
    tiles = half // 128
    big = tiles // 2
    return [128 * w for w in (big, big, tiles - 2 * big) if w]


def fused(
    experts,
    heads,
    span,
    tokens_ref,
    scores_ref,
    routes_ref,
    gate_up_ref,
    down_ref,
    out_ref,
    w_in,
    w_pairs,
    w_out,
    flat,
    packed,
    spread,
    share,
    sums,
    sums_out,
    sums_in,
    hidden_all,
    own,
    tokens_in,
    scores_in,
    routes_in,
    *rest,
):
    parts = (len(rest) - 11) // 2
    results_out, results_in = rest[:parts], rest[parts : 2 * parts]
    (w_sem, down_sem, tok_send, tok_recv, sum_send, sum_recv, hid_send, hid_recv, res_send, res_recv, in_sem) = rest[2 * parts :]
    steps, rows, width = tokens_ref.shape
    half = width // 2
    count = steps * rows
    tiles = w_in.shape[0]
    units = tiles * 128
    chunks = w_pairs.shape[0]
    per_send = sums_out.shape[3] // 256
    groups = experts // heads
    me = lax.axis_index("expert")
    my_head = lax.axis_index("head")

    barrier = pltpu.get_barrier_semaphore()
    for o in range(1, experts):
        pl.semaphore_signal(barrier, inc=1, device_id={"expert": lax.rem(me + o, experts)}, device_id_type=MESH)
    for o in range(1, heads):
        pl.semaphore_signal(barrier, inc=1, device_id={"head": lax.rem(my_head + o, heads)}, device_id_type=MESH)

    small_copies = [
        pltpu.make_async_copy(src, dst, in_sem.at[n])
        for n, (src, dst) in enumerate(((tokens_ref, tokens_in), (scores_ref, scores_in), (routes_ref, routes_in)))
    ]
    for copy in small_copies:
        copy.start()
    weight_copies = [
        pltpu.make_async_copy(gate_up_ref.at[:, 2 * c : 2 * c + 2, :], w_in.at[c], w_sem.at[c]) for c in range(tiles)
    ]
    for copy in weight_copies:
        copy.start()

    small_copies[0].wait()
    for s in range(steps):
        flat[s * rows : (s + 1) * rows, :] = tokens_in[s].astype(F32)
    packed[0] = jnp.concatenate([flat[:, :half], flat[:, half:]], axis=0).astype(BF16)

    pl.semaphore_wait(barrier, experts + heads - 2)

    token_copies = []
    for o in range(1, experts):
        copy = pltpu.make_async_remote_copy(
            src_ref=packed.at[0],
            dst_ref=packed.at[o],
            send_sem=tok_send.at[o],
            recv_sem=tok_recv.at[o],
            device_id={"expert": lax.rem(me + o, experts)},
            device_id_type=MESH,
        )
        copy.start()
        token_copies.append(copy)

    small_copies[1].wait()
    small_copies[2].wait()
    eye = lax.broadcasted_iota(jnp.int32, (rows, rows), 0) == lax.broadcasted_iota(jnp.int32, (rows, rows), 1)
    for s in range(steps):
        scores = scores_in[s]
        weights = 2.5 * scores / jnp.sum(scores, axis=0, keepdims=True)
        for b in range(experts):
            slot = lax.rem(me + b, experts) // span
            row = jnp.sum(jnp.where(routes_in[s] == slot, weights, 0.0), axis=0, keepdims=True)
            column = jnp.sum(jnp.where(eye, jnp.broadcast_to(row, (rows, rows)), 0.0), axis=1, keepdims=True)
            column = jnp.broadcast_to(column, (rows, 128))
            share[b, s * rows : (s + 1) * rows, :] = column
            share[b, count + s * rows : count + (s + 1) * rows, :] = column

    for c in range(chunks):
        weight_copies[2 * c].wait()
        weight_copies[2 * c + 1].wait()
        w_pairs[c] = jnp.concatenate([w_in[2 * c + i].reshape(2 * width, 128) for i in range(2)], axis=1)
    down_copy = pltpu.make_async_copy(down_ref, w_out, down_sem)
    down_copy.start()

    lane = lax.broadcasted_iota(jnp.int32, (128, 512), 1)
    feature = lax.broadcasted_iota(jnp.int32, (128, 512), 0)
    place = jnp.where(lane < 256, 2 * feature, 2 * feature + 257)
    selector = jnp.where(lane == place, 1.0, 0.0).astype(BF16)
    per_half = half // 128
    for b in range(experts):
        if b:
            token_copies[b - 1].wait_recv()
        block = packed[b]
        stack = jnp.concatenate([block[:, 128 * j : 128 * j + 128] for j in range(per_half)], axis=0)
        wide = jnp.dot(stack, selector, preferred_element_type=F32)
        for j in range(per_half):
            for k in range(2):
                piece = wide[16 * j + 8 * k : 16 * j + 8 * k + 8]
                pair = jnp.concatenate([piece[:, :256], piece[:, 256:]], axis=0).astype(BF16)
                at = 256 * (k * per_half + j)
                spread[16 * b : 16 * b + 16, at : at + 256] = pair

    sum_copies = []
    for c in range(chunks):
        part = jnp.dot(spread[...], w_pairs[c], preferred_element_type=F32)
        part = part.reshape(heads, 16 * groups, 256)
        sums[:, :, 256 * c : 256 * c + 256] = part
        n, k = c // per_send, c % per_send
        sums_out[:, n, :, 256 * k : 256 * k + 256] = part.astype(BF16)
        if k == per_send - 1:
            for o in range(1, heads):
                peer = lax.rem(my_head + o, heads)
                copy = pltpu.make_async_remote_copy(
                    src_ref=sums_out.at[peer, n],
                    dst_ref=sums_in.at[o - 1, n],
                    send_sem=sum_send.at[o - 1, n],
                    recv_sem=sum_recv.at[o - 1, n],
                    device_id={"head": peer},
                    device_id_type=MESH,
                )
                copy.start()
                sum_copies.append(copy)

    for copy in sum_copies:
        copy.wait_recv()
    sends = sums_out.shape[1]
    total = sums[my_head]
    for o in range(1, heads):
        total += jnp.concatenate([sums_in[o - 1, n].astype(F32) for n in range(sends)], axis=1)
    total = total.reshape(groups, 2, 8, units)
    gate, up = total[:, 0], total[:, 1]
    hidden = gate / (1.0 + jnp.exp(-gate)) * up
    hidden = jnp.stack([hidden[:, :, : units // 2], hidden[:, :, units // 2 :]], axis=1)
    hidden_all[my_head] = hidden.reshape(16 * groups, units // 2).astype(BF16)
    hidden_copies = []
    for o in range(1, heads):
        copy = pltpu.make_async_remote_copy(
            src_ref=hidden_all.at[my_head],
            dst_ref=hidden_all.at[my_head],
            send_sem=hid_send.at[o - 1],
            recv_sem=hid_recv.at[o - 1],
            device_id={"head": lax.rem(my_head + o, heads)},
            device_id_type=MESH,
        )
        copy.start()
        hidden_copies.append(copy)
    down_copy.wait()
    for copy in hidden_copies:
        copy.wait_recv()

    blocks = hidden_all[...].astype(F32).reshape(experts, 2, 8, units // 2)
    left = jnp.concatenate([blocks[:, 0], blocks[:, 1]], axis=2).reshape(8 * experts, units).astype(BF16)
    result_copies = []
    at = 0
    for n in range(parts):
        size = results_out[n].shape[2]
        low = jnp.dot(left, w_out[:, at : at + size], preferred_element_type=F32)
        high = jnp.dot(left, w_out[:, half + at : half + at + size], preferred_element_type=F32)
        both = jnp.concatenate([low.reshape(experts, 8, size), high.reshape(experts, 8, size)], axis=1)
        own[:, at : at + size] = both[0]
        results_out[n][...] = both.astype(BF16)
        for b in range(1, experts):
            copy = pltpu.make_async_remote_copy(
                src_ref=results_out[n].at[b],
                dst_ref=results_in[n].at[b],
                send_sem=res_send.at[b, n],
                recv_sem=res_recv.at[b, n],
                device_id={"expert": lax.rem(me - b + experts, experts)},
                device_id_type=MESH,
            )
            copy.start()
            result_copies.append(copy)
        at += size

    at = 0
    for n in range(parts):
        size = results_out[n].shape[2]
        mixed = share[0][:, :1] * own[:, at : at + size]
        for b in range(1, experts):
            result_copies[n * (experts - 1) + b - 1].wait_recv()
            mixed += share[b][:, :1] * results_in[n][b].astype(F32)
        for s in range(steps):
            for k in range(2):
                rows_at = k * count + s * rows
                to = k * half + at
                out_ref[s, :, to : to + size] = mixed[rows_at : rows_at + rows].astype(BF16)
        at += size

    for copy in token_copies + sum_copies + hidden_copies + result_copies:
        copy.wait_send()


def body(experts, heads, tokens, gate_scores, route_copy, gate_up, down_proj):
    steps, rows, width = tokens.shape
    units = gate_up.shape[3]
    span = max(1, experts // 16)
    count = steps * rows
    half = width // 2
    tiles = units // 128
    chunks = units // 256
    groups = experts // heads
    per_send = min(2, chunks)
    sends = chunks // per_send
    assert count == 8 and experts % heads == 0 and units % 256 == 0 and half % 128 == 0
    gate_up = gate_up.reshape(width, 2, tiles, 128).transpose(0, 2, 1, 3).reshape(width, 2 * tiles, 128)
    down = down_proj.reshape(units, width)
    parts = widths_of(half)
    vmem, hbm = pl.BlockSpec(memory_space=pltpu.VMEM), pl.BlockSpec(memory_space=pl.ANY)
    dma = pltpu.SemaphoreType.DMA
    flops = 2 * 8 * experts * width * units * 3
    return pl.pallas_call(
        functools.partial(fused, experts, heads, span),
        out_shape=jax.ShapeDtypeStruct(tokens.shape, tokens.dtype),
        in_specs=[hbm] * 5,
        out_specs=vmem,
        scratch_shapes=[
            pltpu.VMEM((tiles, width, 2, 128), BF16),
            pltpu.VMEM((chunks, 2 * width, 256), BF16),
            pltpu.VMEM((units, width), BF16),
            pltpu.VMEM((8, width), F32),
            pltpu.VMEM((experts, 16, half), BF16),
            pltpu.VMEM((16 * experts, 2 * width), BF16),
            pltpu.VMEM((experts, 16, 128), F32),
            pltpu.VMEM((heads, 16 * groups, units), F32),
            pltpu.VMEM((heads, sends, 16 * groups, 256 * per_send), BF16),
            pltpu.VMEM((heads - 1, sends, 16 * groups, 256 * per_send), BF16),
            pltpu.VMEM((heads, 16 * groups, units // 2), BF16),
            pltpu.VMEM((16, half), F32),
            pltpu.VMEM(tokens.shape, BF16),
            pltpu.VMEM((steps, route_copy.shape[2], rows), F32),
            pltpu.VMEM((steps, route_copy.shape[2], rows), jnp.int32),
        ]
        + [pltpu.VMEM((experts, 16, size), BF16) for size in parts] * 2
        + [
            dma((tiles,)),
            dma,
            dma((experts,)),
            dma((experts,)),
            dma((heads - 1, sends)),
            dma((heads - 1, sends)),
            dma((heads - 1,)),
            dma((heads - 1,)),
            dma((experts, len(parts))),
            dma((experts, len(parts))),
            dma((3,)),
        ],
        compiler_params=pltpu.CompilerParams(
            collective_id=0, has_side_effects=True, vmem_limit_bytes=56 * 2**20
        ),
        cost_estimate=pl.CostEstimate(
            flops=flops, bytes_accessed=6 * width * units, transcendentals=8 * groups * units
        ),
    )(tokens, gate_scores.transpose(0, 2, 1), route_copy.transpose(0, 2, 1), gate_up, down)


def solution(mesh):
    experts, heads = mesh.shape["expert"], mesh.shape["head"]
    return jax.shard_map(
        functools.partial(body, experts, heads),
        mesh=mesh,
        in_specs=(
            P(None, ("groups", "expert"), "head"),
            P(None, ("groups", "expert"), None),
            P(None, ("groups", "expert"), None),
            P("expert", "head", None, None),
            P("expert", None, "head"),
        ),
        out_specs=P(None, ("groups", "expert"), "head"),
        check_vma=False,
    )
```
